32 devices in a mesh: stn: 2 (over x), tm: 16 (over z, y, core).
Axes of the slice: x: 2, y: 2, z: 4, core: 2. Of those that a mesh axis runs over, the one named last changes fastest.
Arguments:
- voltages: bfloat16 [64, 2, 32, 8192], P('stn', None, None, 'tm'), may hold values from -6 to 6
- phase_codes: int32 [64, 32, 64], replicated, may hold values from 0 to 255
- dispersion: int32 [64], replicated, may hold values from 1 to 4095
Outputs:
- dedispersed: float32 [64, 2, 32, 8192], P('stn', None, None, 'tm')
The draws below stay inside these ranges and needn't reach their ends.
All inputs are finite; a program needn't handle non-finite values.
Results may differ from the reference program's by a relative error of at most 0.0003.
Values may be sent and summed in bfloat16 or wider, within the bound.
A program may use at most 128 MiB of HBM per device.

```python
import math
import jax
import jax.numpy as jnp
from jax import lax

BEAMS = 64
CHANS = 32
STATIONS = 64
TIME = 8192


def set_ends(values, own_key, least, high):
    longest = values.shape.index(max(values.shape))
    spots = []
    for shift in (0, 1):
        where = [jax.random.randint(jax.random.fold_in(own_key, axis), (), 0, length) for axis, length in enumerate(values.shape)]
        where[longest] = (where[longest] + shift) % values.shape[longest]
        spots.append(tuple(where))
    return values.at[spots[0]].set(least).at[spots[1]].set(high)


def level_of(key, dims, split, smallest, high):
    factor_of = 1.0
    for position, parts in split:
        heights = jax.random.uniform(jax.random.fold_in(jax.random.fold_in(key, 6), position), (parts,), jnp.float32, smallest / len(split), high / len(split))
        factor_of = factor_of * jnp.repeat(jnp.exp(heights), dims[position] // parts).reshape((-1,) + (1,) * (len(dims) - 1 - position))
    return factor_of


def scatter_about(rng, extent, scale, reach, shards=(), kind=jnp.bfloat16):
    gain = level_of(rng, extent, shards, -0.22, 0.18) if shards else 1.0
    values = jax.random.normal(rng, extent, jnp.float32) * scale * gain
    return jnp.minimum(jnp.maximum(values, -reach), reach).astype(kind)


def setup_inputs(seed: int = 0) -> dict:
    seeds = jax.random.split(jax.random.key(seed), 4)
    return {
        "voltages": scatter_about(seeds[0], (STATIONS, 2, CHANS, TIME), 1.0, 6.0, ((0, 2), (3, 16))),
        "phase_codes": set_ends(jax.random.randint(seeds[1], (STATIONS, CHANS, BEAMS), 0, 256), jax.random.fold_in(seeds[1], 1), 0, 255).astype(jnp.int32),
        "dispersion": set_ends(jax.random.randint(seeds[2], (BEAMS,), 1, 4096), jax.random.fold_in(seeds[2], 1), 1, 4095).astype(jnp.int32),
    }


chirp_modulus = 4096
phase_levels = 256

def weight_parts(phase_codes, weight_scale):
    angles = phase_codes.astype(jnp.float32) * (2.0 * math.pi / phase_levels)
    return (jnp.cos(angles) * weight_scale, jnp.sin(angles) * weight_scale)

def reference(voltages, phase_codes, dispersion):
    weight_scale = 1.0 / math.sqrt(STATIONS)
    w_real, w_imaginary = weight_parts(phase_codes, weight_scale)

    def contract(left, right):
        return jnp.einsum('sb,st->bt', left, right, precision=lax.Precision.HIGHEST)

    def one_channel(channel):
        wr_part = lax.dynamic_index_in_dim(w_real, channel, 1, keepdims=False)
        wi_part = lax.dynamic_index_in_dim(w_imaginary, channel, 1, keepdims=False)
        channel_block = lax.dynamic_index_in_dim(voltages, channel, 2, keepdims=False).astype(jnp.float32)
        volt_real = channel_block[:, 0]
        volt_imaginary = channel_block[:, 1]
        beam_real = contract(wr_part, volt_real) - contract(wi_part, volt_imaginary)
        beam_imaginary = contract(wr_part, volt_imaginary) + contract(wi_part, volt_real)
        return (beam_real, beam_imaginary)
    beam_real, beam_imaginary = lax.map(one_channel, jnp.arange(CHANS, dtype=jnp.int32))
    beam_real = jnp.transpose(beam_real, (1, 0, 2))
    beam_imaginary = jnp.transpose(beam_imaginary, (1, 0, 2))
    sample_ids = jnp.arange(TIME, dtype=jnp.int32)
    centered = jnp.where(sample_ids < TIME // 2, sample_ids, sample_ids - TIME)
    squares = centered * centered % chirp_modulus
    rates = 2 * CHANS - jnp.arange(CHANS, dtype=jnp.int32)

    def one_beam(operands):
        real_part, imaginary, measure = operands
        spectrum = jnp.fft.fft(lax.complex(real_part, imaginary), axis=-1)
        chirp_rate = measure * rates % chirp_modulus
        phase_index = chirp_rate[:, None] * squares[None, :] % chirp_modulus
        angles = phase_index.astype(jnp.float32) * (-2.0 * math.pi / chirp_modulus)
        spectrum = spectrum * lax.complex(jnp.cos(angles), jnp.sin(angles))
        series = jnp.fft.ifft(spectrum, axis=-1)
        return jnp.stack([jnp.real(series), jnp.imag(series)], axis=0)
    result = lax.map(one_beam, (beam_real, beam_imaginary, dispersion))
    return result.astype(jnp.float32)
```

```python
import functools
import math

import jax
import jax.numpy as jnp
import ml_dtypes
import numpy as np
from jax import lax
from jax.experimental import pallas as pl
from jax.experimental.pallas import tpu as pltpu
from jax.sharding import PartitionSpec as P

chirp_modulus = 4096
phase_levels = 256


def weight_stack(phase_codes, weight_scale):
    angles = phase_codes.astype(jnp.float32) * (2.0 * math.pi / phase_levels)
    w_real = jnp.cos(angles) * weight_scale
    w_imaginary = jnp.sin(angles) * weight_scale
    return jnp.stack([w_real, w_imaginary], axis=1)


def shard_terms(weights, voltages):
    wr_part = weights[:, 0]
    wi_part = weights[:, 1]
    volt_real = voltages[:, 0]
    volt_imaginary = voltages[:, 1]

    def contract(left, right):
        return jnp.einsum(
            "scb,sct->bct",
            left,
            right,
            preferred_element_type=jnp.float32,
            precision=lax.Precision.HIGHEST,
        )

    real_part = contract(wr_part, volt_real) - contract(wi_part, volt_imaginary)
    imaginary = contract(wr_part, volt_imaginary) + contract(wi_part, volt_real)
    return jnp.stack([real_part, imaginary], axis=1)


def angle_pair(row_ids, column_ids, modulus, direction):
    phase_index = row_ids[:, None] * column_ids[None, :] % modulus
    angles = phase_index.astype(jnp.float32) * (direction * 2.0 * math.pi / modulus)
    return (jnp.cos(angles), jnp.sin(angles))


def along_last(real_part, imaginary, tables):
    cos_part, sin_part = tables

    def contract(left, right):
        return jnp.einsum("...n,nk->...k", left, right, precision=lax.Precision.HIGHEST)

    return (
        contract(real_part, cos_part) - contract(imaginary, sin_part),
        contract(real_part, sin_part) + contract(imaginary, cos_part),
    )


def along_second(real_part, imaginary, tables):
    cos_part, sin_part = tables

    def contract(left, right):
        return jnp.einsum("...nl,nk->...kl", left, right, precision=lax.Precision.HIGHEST)

    return (
        contract(real_part, cos_part) - contract(imaginary, sin_part),
        contract(real_part, sin_part) + contract(imaginary, cos_part),
    )


def rotate(real_part, imaginary, tables):
    cos_part, sin_part = tables
    return (
        real_part * cos_part - imaginary * sin_part,
        real_part * sin_part + imaginary * cos_part,
    )


def chirp_pair(dm_values, channel_ids, frequency, length, channel_total):
    centered = jnp.where(frequency < length // 2, frequency, frequency - length)
    squares = centered * centered % chirp_modulus
    chirp_rate = dm_values[:, None] * (2 * channel_total - channel_ids)[None, :] % chirp_modulus
    phase_index = chirp_rate[:, :, None, None] * squares[None, None] % chirp_modulus
    angles = phase_index.astype(jnp.float32) * (-2.0 * math.pi / chirp_modulus)
    return (jnp.cos(angles), jnp.sin(angles))


def body(voltages, phase_codes, dispersion):
    stn_count = lax.axis_size("stn")
    group_size = voltages.shape[0]
    channels = voltages.shape[2]
    local_time = voltages.shape[3]
    beam_total = phase_codes.shape[2]
    station_total = phase_codes.shape[0]
    own_beams = beam_total // stn_count
    own_start = lax.axis_index("stn") * own_beams
    weight_scale = 1.0 / math.sqrt(station_total)
    group_start = lax.axis_index("stn") * group_size
    local_codes = lax.dynamic_slice_in_dim(phase_codes, group_start, group_size, 0)
    weights = weight_stack(local_codes, weight_scale)
    beams = lax.psum_scatter(shard_terms(weights, voltages), "stn", scatter_dimension=0, tiled=True)
    time_shards = lax.axis_size("tm")
    time_rank = lax.axis_index("tm")
    length = time_shards * local_time
    shard_ids = jnp.arange(time_shards, dtype=jnp.int32)
    sample_ids = jnp.arange(local_time, dtype=jnp.int32)
    dm_values = lax.dynamic_slice_in_dim(dispersion, own_start, own_beams)
    inverse_length = 1.0 / length
    column_width = local_time // time_shards
    layout = beams.reshape(own_beams, 2, channels, 1, local_time)
    layout = lax.all_to_all(layout, "tm", split_axis=4, concat_axis=3, tiled=True)
    real_part, imaginary = along_second(
        layout[:, 0], layout[:, 1], angle_pair(shard_ids, shard_ids, time_shards, -1.0)
    )
    global_samples = time_rank * column_width + jnp.arange(column_width, dtype=jnp.int32)
    real_part, imaginary = rotate(
        real_part, imaginary, angle_pair(shard_ids, global_samples, length, -1.0)
    )
    layout = lax.all_to_all(
        jnp.stack([real_part, imaginary], axis=1), "tm", split_axis=3, concat_axis=4, tiled=True
    )
    real_part, imaginary = along_last(
        layout[:, 0], layout[:, 1], angle_pair(sample_ids, sample_ids, local_time, -1.0)
    )
    frequency = time_rank + time_shards * sample_ids[None, :]
    channel_ids = jnp.arange(channels, dtype=jnp.int32)
    real_part, imaginary = rotate(
        real_part, imaginary, chirp_pair(dm_values, channel_ids, frequency, length, channels)
    )
    real_part, imaginary = along_last(
        real_part, imaginary, angle_pair(sample_ids, sample_ids, local_time, 1.0)
    )
    rank_ids = jnp.reshape(time_rank, (1,))
    real_part, imaginary = rotate(
        real_part, imaginary, angle_pair(rank_ids, sample_ids, length, 1.0)
    )
    layout = lax.all_to_all(
        jnp.stack([real_part, imaginary], axis=1), "tm", split_axis=4, concat_axis=3, tiled=True
    )
    real_part, imaginary = along_second(
        layout[:, 0], layout[:, 1], angle_pair(shard_ids, shard_ids, time_shards, 1.0)
    )
    layout = jnp.stack([real_part, imaginary], axis=1) * inverse_length
    layout = lax.all_to_all(layout, "tm", split_axis=3, concat_axis=4, tiled=True)
    return layout.reshape(own_beams, 2, channels, local_time)


MESH = pl.DeviceIdType.MESH
base_length = chirp_modulus // 2
lane_count = 128
code_limit = 32766.0


def split_pair(values):
    high = values.astype(jnp.bfloat16)
    return high, (values - high.astype(jnp.float32)).astype(jnp.bfloat16)


def host_split(values):
    high = values.astype(ml_dtypes.bfloat16)
    low = (values - high.astype(np.float64)).astype(ml_dtypes.bfloat16)
    return np.stack([high, low])


def lane_tables():
    ids = np.arange(lane_count)
    angles = 2.0 * np.pi * (np.outer(ids, ids) % lane_count) / lane_count
    cos_part, sin_part = np.cos(angles), np.sin(angles)
    forward = np.block([[cos_part, -sin_part], [sin_part, cos_part]])
    inverse = np.block([[cos_part, sin_part], [-sin_part, cos_part]]) / base_length
    return host_split(forward), host_split(inverse)


def twiddle_table(parts):
    angles = 2.0 * np.pi * np.outer(np.arange(parts), np.arange(lane_count)) / base_length
    return np.stack([np.cos(angles), np.sin(angles)]).astype(np.float32)


def lane_order(width):
    strands = width // lane_count
    order = np.zeros((width, width), np.float32)
    for sample in range(width):
        order[sample, (sample % strands) * lane_count + sample // strands] = 1.0
    return order.astype(ml_dtypes.bfloat16)


def times_root(value, step, count, direction):
    real_part, imaginary = value
    if step == 0:
        return value
    if 4 * step == count:
        return (-imaginary, real_part) if direction > 0 else (imaginary, -real_part)
    cosine = math.cos(2.0 * math.pi * step / count)
    sine = direction * math.sin(2.0 * math.pi * step / count)
    return (real_part * cosine - imaginary * sine, real_part * sine + imaginary * cosine)


def short_transform(values, direction):
    count = len(values)
    if count == 1:
        return values
    even = short_transform(values[0::2], direction)
    odd = short_transform(values[1::2], direction)
    low, high = [], []
    for step in range(count // 2):
        turned = times_root(odd[step], step, count, direction)
        low.append((even[step][0] + turned[0], even[step][1] + turned[1]))
        high.append((even[step][0] - turned[0], even[step][1] - turned[1]))
    return low + high


def unit_circle(index):
    quarter = chirp_modulus // 4
    turns = lax.shift_right_arithmetic(index + quarter // 2, quarter.bit_length() - 1)
    theta = (index - turns * quarter).astype(jnp.float32) * (2.0 * math.pi / chirp_modulus)
    square = theta * theta
    sine = theta * (1.0 + square * (-1 / 6 + square * (1 / 120 + square * (-1 / 5040 + square * (1 / 362880)))))
    cosine = 1.0 + square * (-1 / 2 + square * (1 / 24 + square * (-1 / 720 + square * (1 / 40320 - square / 3628800))))
    swap = (turns & 1) == 1
    first = jnp.where(swap, sine, cosine)
    second = jnp.where(swap, cosine, sine)
    first = jnp.where(((turns + 1) & 2) == 2, -first, first)
    second = jnp.where((turns & 2) == 2, -second, second)
    return first, second


def dot(left, right):
    return jnp.dot(left, right, preferred_element_type=jnp.float32)


def dot_split(left, table_ref):
    high, low = split_pair(left)
    return dot(high, table_ref[0]) + dot(low, table_ref[0]) + dot(high, table_ref[1])


def filter_kernel(
    stn_count, parts, volt_ref, weight_ref, rate_ref, order_ref, back_ref, fwd_ref, inv_ref, twiddle_ref,
    out_ref, scale_ref, grid_ref, mid_ref, chirp_ref,
):
    width = volt_ref.shape[2]
    strands = width // lane_count
    beams = rate_ref.shape[0]
    own_beams = beams // stn_count
    rows = 8
    chunk = 4
    weight_high, weight_low = split_pair(weight_ref[...])

    @pl.loop(0, parts)
    def _(part):
        pieces = [volt_ref[stn * parts + part] for stn in range(stn_count)]
        block = jnp.concatenate(pieces, axis=0)
        block = dot(block, order_ref[...]).astype(jnp.bfloat16)
        grid_ref[part] = dot(weight_high, block) + dot(weight_low, block)

    def tile(step):
        group, strand = step // strands, step % strands
        return (
            pl.ds(pl.multiple_of(group * rows, rows), rows),
            pl.ds(pl.multiple_of(beams + group * rows, rows), rows),
            pl.ds(pl.multiple_of(strand * lane_count, lane_count), lane_count),
            strand,
        )

    @pl.loop(0, beams // rows * strands)
    def _(step):
        top, bottom, lanes, strand = tile(step)
        values = [(grid_ref[p, top, lanes], grid_ref[p, bottom, lanes]) for p in range(parts)]
        for k, (real_part, imaginary) in enumerate(short_transform(values, -1)):
            cosine, sine = twiddle_ref[0, pl.ds(k, 1)], twiddle_ref[1, pl.ds(k, 1)]
            mid_ref[strand, k, top, :lane_count] = real_part * cosine + imaginary * sine
            mid_ref[strand, k, top, lane_count:] = imaginary * cosine - real_part * sine

    rates = rate_ref[...]

    @pl.loop(0, parts)
    def _(part):
        column = lax.broadcasted_iota(jnp.int32, (beams, lane_count), 1)
        frequency = part + parts * column
        squares = (frequency * frequency) & (chirp_modulus - 1)
        index = (rates * squares) & (chirp_modulus - 1)
        cosine, sine = unit_circle(index)
        chirp_ref[0, part] = cosine
        chirp_ref[1, part] = sine

    groups = parts // chunk

    @pl.loop(0, strands * groups)
    def _(step):
        strand, first = step // groups, (step % groups) * chunk
        some = pl.ds(first, chunk)
        spectrum = dot_split(mid_ref[strand, some].reshape(chunk * beams, 2 * lane_count), fwd_ref)
        real_part, imaginary = spectrum[:, :lane_count], spectrum[:, lane_count:]
        cosine = chirp_ref[0, some].reshape(chunk * beams, lane_count)
        sine = chirp_ref[1, some].reshape(chunk * beams, lane_count)
        turned = jnp.concatenate(
            [real_part * cosine + imaginary * sine, imaginary * cosine - real_part * sine], axis=1
        )
        mid_ref[strand, some] = dot_split(turned, inv_ref).reshape(chunk, beams, 2 * lane_count)

    @pl.loop(0, beams // rows * strands)
    def _(step):
        top, bottom, lanes, strand = tile(step)
        values = []
        for k in range(parts):
            cosine, sine = twiddle_ref[0, pl.ds(k, 1)], twiddle_ref[1, pl.ds(k, 1)]
            real_part = mid_ref[strand, k, top, :lane_count]
            imaginary = mid_ref[strand, k, top, lane_count:]
            values.append((real_part * cosine - imaginary * sine, real_part * sine + imaginary * cosine))
        for p, (real_part, imaginary) in enumerate(short_transform(values, 1)):
            grid_ref[p, top, lanes] = real_part
            grid_ref[p, bottom, lanes] = imaginary

    row_ids = lax.broadcasted_iota(jnp.int32, (own_beams, lane_count), 0)
    lane_ids = lax.broadcasted_iota(jnp.int32, (own_beams, lane_count), 1)

    @pl.loop(0, parts)
    def _(part):
        high, low = split_pair(grid_ref[part])
        series = dot(high, back_ref[...]) + dot(low, back_ref[...])
        peak = jnp.maximum(jnp.max(jnp.abs(series), axis=1, keepdims=True), 1e-30)
        codes = jnp.round(series * (code_limit / peak)).astype(jnp.int32)
        words = (codes[:beams] << 16) | (codes[beams:] & 0xFFFF)
        for stn in range(stn_count):
            slot = stn * parts + part
            first = stn * own_beams
            out_ref[slot] = words[first : first + own_beams]
            peaks = jnp.where(row_ids == lane_ids, peak[first : first + own_beams], 0.0)
            second = beams + first
            peaks += jnp.where(
                row_ids + own_beams == lane_ids, peak[second : second + own_beams], 0.0
            )
            peaks = jnp.sum(peaks, axis=0, keepdims=True)
            scale_ref[slot] = jnp.broadcast_to(peaks, scale_ref.shape[1:])


def filter_channel(stn_count, parts, volts, weights, rates):
    devices, _, width = volts.shape
    beams = rates.shape[0]
    forward, inverse = lane_tables()
    order = lane_order(width)
    vmem = pl.BlockSpec(memory_space=pltpu.VMEM)
    return pl.pallas_call(
        functools.partial(filter_kernel, stn_count, parts),
        out_shape=(
            jax.ShapeDtypeStruct((devices, beams // stn_count, width), jnp.int32),
            jax.ShapeDtypeStruct((devices, 8, lane_count), jnp.float32),
        ),
        in_specs=[vmem] * 8,
        out_specs=(vmem, vmem),
        scratch_shapes=[
            pltpu.VMEM((parts, 2 * beams, width), jnp.float32),
            pltpu.VMEM((width // lane_count, parts, beams, 2 * lane_count), jnp.float32),
            pltpu.VMEM((2, parts, beams, lane_count), jnp.float32),
        ],
        compiler_params=pltpu.CompilerParams(vmem_limit_bytes=40 * 2**20),
        name="filter_channel",
    )(
        volts, weights, rates, jnp.asarray(order), jnp.asarray(order.T), jnp.asarray(forward),
        jnp.asarray(inverse), jnp.asarray(twiddle_table(parts)),
    )


def exchange_kernel(stn_count, parts, count, *refs):
    ins, outs = refs[:count], refs[count : 2 * count]
    send_sems, recv_sems, copy_sems = refs[2 * count :]
    devices = stn_count * parts
    me = lax.axis_index("stn") * parts + lax.axis_index("tm")

    def place(device):
        return (device // parts, device % parts)

    def remote(which, offset, target, slot):
        return pltpu.make_async_remote_copy(
            src_ref=ins[which].at[target],
            dst_ref=outs[which].at[slot],
            send_sem=send_sems.at[which, offset],
            recv_sem=recv_sems.at[which, offset],
            device_id=place(target),
            device_id_type=MESH,
        )

    barrier = pltpu.get_barrier_semaphore()

    @pl.loop(1, devices)
    def _(offset):
        pl.semaphore_signal(
            barrier, inc=1, device_id=place(lax.rem(me + offset, devices)), device_id_type=MESH
        )

    pl.semaphore_wait(barrier, devices - 1)

    @pl.loop(1, devices)
    def _(offset):
        target = lax.rem(me + offset, devices)
        for which in range(count):
            remote(which, offset, target, me).start()

    own = [
        pltpu.make_async_copy(ins[which].at[me], outs[which].at[me], copy_sems.at[which])
        for which in range(count)
    ]
    for copy in own:
        copy.start()
    for copy in own:
        copy.wait()

    @pl.loop(1, devices)
    def _(offset):
        target = lax.rem(me + offset, devices)
        origin = lax.rem(me + devices - offset, devices)
        for which in range(count):
            remote(which, offset, target, me).wait_send()
            remote(which, offset, target, origin).wait_recv()


def exchange(stn_count, parts, arrays, collective_id):
    devices = stn_count * parts
    count = len(arrays)
    place = pl.BlockSpec(memory_space=pl.ANY)
    return pl.pallas_call(
        functools.partial(exchange_kernel, stn_count, parts, count),
        out_shape=tuple(
            jax.ShapeDtypeStruct(x.shape, x.dtype) for x in arrays
        ),
        in_specs=[place] * count,
        out_specs=(place,) * count,
        scratch_shapes=[
            pltpu.SemaphoreType.DMA((count, devices)),
            pltpu.SemaphoreType.DMA((count, devices)),
            pltpu.SemaphoreType.DMA((count,)),
        ],
        compiler_params=pltpu.CompilerParams(collective_id=collective_id, has_side_effects=True),
        name="exchange_%d" % collective_id,
    )(*arrays)


def channel_body(voltages, phase_codes, dispersion):
    stn_count, parts = lax.axis_size("stn"), lax.axis_size("tm")
    group_size, _, channels, width = voltages.shape
    station_total, _, beams = phase_codes.shape
    channel = lax.axis_index("stn") * parts + lax.axis_index("tm")
    sent = jnp.transpose(voltages, (2, 0, 1, 3)).reshape(channels, 2 * group_size, width)
    (volts,) = exchange(stn_count, parts, [sent], 0)
    codes = lax.dynamic_index_in_dim(phase_codes, channel, 1, keepdims=False).T
    angles = codes.astype(jnp.float32) * (2.0 * math.pi / phase_levels)
    w_real = jnp.cos(angles) / math.sqrt(station_total)
    w_imaginary = jnp.sin(angles) / math.sqrt(station_total)
    weights = jnp.stack(
        [jnp.stack([w_real, -w_imaginary], axis=-1), jnp.stack([w_imaginary, w_real], axis=-1)]
    ).reshape(2 * beams, 2 * station_total)
    rates = (dispersion * (2 * channels - channel) % chirp_modulus)[:, None]
    words, peaks = filter_channel(stn_count, parts, volts, weights, rates)
    words, peaks = exchange(stn_count, parts, [words, peaks], 1)
    own_beams = beams // stn_count
    codes = jnp.stack([words >> 16, (words << 16) >> 16], axis=1).astype(jnp.float32)
    steps = peaks[:, 0, : 2 * own_beams].reshape(channels, 2, own_beams, 1) * (1.0 / code_limit)
    return jnp.transpose(codes * steps, (2, 1, 0, 3))


def solution(mesh):
    stn_count, parts = mesh.shape["stn"], mesh.shape["tm"]

    def run(voltages, phase_codes, dispersion):
        channels, length = voltages.shape[2:]
        by_channel = channels == stn_count * parts and parts * lane_count == base_length
        by_channel = by_channel and length % base_length == 0
        return jax.shard_map(
            channel_body if by_channel else body,
            mesh=mesh,
            in_specs=(P("stn", None, None, "tm"), P(), P()),
            out_specs=P("stn", None, None, "tm"),
            check_vma=False,
        )(voltages, phase_codes, dispersion)

    return run
```

```python
import functools
import math

import jax
import jax.numpy as jnp
import ml_dtypes
import numpy as np
from jax import lax
from jax.experimental import pallas as pl
from jax.experimental.pallas import tpu as pltpu
from jax.sharding import PartitionSpec as P

chirp_modulus = 4096
phase_levels = 256


def weight_stack(phase_codes, weight_scale):
    angles = phase_codes.astype(jnp.float32) * (2.0 * math.pi / phase_levels)
    w_real = jnp.cos(angles) * weight_scale
    w_imaginary = jnp.sin(angles) * weight_scale
    return jnp.stack([w_real, w_imaginary], axis=1)


def shard_terms(weights, voltages):
    wr_part = weights[:, 0]
    wi_part = weights[:, 1]
    volt_real = voltages[:, 0]
    volt_imaginary = voltages[:, 1]

    def contract(left, right):
        return jnp.einsum(
            "scb,sct->bct",
            left,
            right,
            preferred_element_type=jnp.float32,
            precision=lax.Precision.HIGHEST,
        )

    real_part = contract(wr_part, volt_real) - contract(wi_part, volt_imaginary)
    imaginary = contract(wr_part, volt_imaginary) + contract(wi_part, volt_real)
    return jnp.stack([real_part, imaginary], axis=1)


def angle_pair(row_ids, column_ids, modulus, direction):
    phase_index = row_ids[:, None] * column_ids[None, :] % modulus
    angles = phase_index.astype(jnp.float32) * (direction * 2.0 * math.pi / modulus)
    return (jnp.cos(angles), jnp.sin(angles))


def along_last(real_part, imaginary, tables):
    cos_part, sin_part = tables

    def contract(left, right):
        return jnp.einsum("...n,nk->...k", left, right, precision=lax.Precision.HIGHEST)

    return (
        contract(real_part, cos_part) - contract(imaginary, sin_part),
        contract(real_part, sin_part) + contract(imaginary, cos_part),
    )


def along_second(real_part, imaginary, tables):
    cos_part, sin_part = tables

    def contract(left, right):
        return jnp.einsum("...nl,nk->...kl", left, right, precision=lax.Precision.HIGHEST)

    return (
        contract(real_part, cos_part) - contract(imaginary, sin_part),
        contract(real_part, sin_part) + contract(imaginary, cos_part),
    )


def rotate(real_part, imaginary, tables):
    cos_part, sin_part = tables
    return (
        real_part * cos_part - imaginary * sin_part,
        real_part * sin_part + imaginary * cos_part,
    )


def chirp_pair(dm_values, channel_ids, frequency, length, channel_total):
    centered = jnp.where(frequency < length // 2, frequency, frequency - length)
    squares = centered * centered % chirp_modulus
    chirp_rate = dm_values[:, None] * (2 * channel_total - channel_ids)[None, :] % chirp_modulus
    phase_index = chirp_rate[:, :, None, None] * squares[None, None] % chirp_modulus
    angles = phase_index.astype(jnp.float32) * (-2.0 * math.pi / chirp_modulus)
    return (jnp.cos(angles), jnp.sin(angles))


def body(voltages, phase_codes, dispersion):
    stn_count = lax.axis_size("stn")
    group_size = voltages.shape[0]
    channels = voltages.shape[2]
    local_time = voltages.shape[3]
    beam_total = phase_codes.shape[2]
    station_total = phase_codes.shape[0]
    own_beams = beam_total // stn_count
    own_start = lax.axis_index("stn") * own_beams
    weight_scale = 1.0 / math.sqrt(station_total)
    group_start = lax.axis_index("stn") * group_size
    local_codes = lax.dynamic_slice_in_dim(phase_codes, group_start, group_size, 0)
    weights = weight_stack(local_codes, weight_scale)
    beams = lax.psum_scatter(shard_terms(weights, voltages), "stn", scatter_dimension=0, tiled=True)
    time_shards = lax.axis_size("tm")
    time_rank = lax.axis_index("tm")
    length = time_shards * local_time
    shard_ids = jnp.arange(time_shards, dtype=jnp.int32)
    sample_ids = jnp.arange(local_time, dtype=jnp.int32)
    dm_values = lax.dynamic_slice_in_dim(dispersion, own_start, own_beams)
    inverse_length = 1.0 / length
    column_width = local_time // time_shards
    layout = beams.reshape(own_beams, 2, channels, 1, local_time)
    layout = lax.all_to_all(layout, "tm", split_axis=4, concat_axis=3, tiled=True)
    real_part, imaginary = along_second(
        layout[:, 0], layout[:, 1], angle_pair(shard_ids, shard_ids, time_shards, -1.0)
    )
    global_samples = time_rank * column_width + jnp.arange(column_width, dtype=jnp.int32)
    real_part, imaginary = rotate(
        real_part, imaginary, angle_pair(shard_ids, global_samples, length, -1.0)
    )
    layout = lax.all_to_all(
        jnp.stack([real_part, imaginary], axis=1), "tm", split_axis=3, concat_axis=4, tiled=True
    )
    real_part, imaginary = along_last(
        layout[:, 0], layout[:, 1], angle_pair(sample_ids, sample_ids, local_time, -1.0)
    )
    frequency = time_rank + time_shards * sample_ids[None, :]
    channel_ids = jnp.arange(channels, dtype=jnp.int32)
    real_part, imaginary = rotate(
        real_part, imaginary, chirp_pair(dm_values, channel_ids, frequency, length, channels)
    )
    real_part, imaginary = along_last(
        real_part, imaginary, angle_pair(sample_ids, sample_ids, local_time, 1.0)
    )
    rank_ids = jnp.reshape(time_rank, (1,))
    real_part, imaginary = rotate(
        real_part, imaginary, angle_pair(rank_ids, sample_ids, length, 1.0)
    )
    layout = lax.all_to_all(
        jnp.stack([real_part, imaginary], axis=1), "tm", split_axis=4, concat_axis=3, tiled=True
    )
    real_part, imaginary = along_second(
        layout[:, 0], layout[:, 1], angle_pair(shard_ids, shard_ids, time_shards, 1.0)
    )
    layout = jnp.stack([real_part, imaginary], axis=1) * inverse_length
    layout = lax.all_to_all(layout, "tm", split_axis=3, concat_axis=4, tiled=True)
    return layout.reshape(own_beams, 2, channels, local_time)


MESH = pl.DeviceIdType.MESH
base_length = chirp_modulus // 2
lane_count = 128
code_limit = 32766.0
halves = 2


def split_pair(values):
    high = values.astype(jnp.bfloat16)
    return high, (values - high.astype(jnp.float32)).astype(jnp.bfloat16)


def host_split(values):
    high = values.astype(ml_dtypes.bfloat16)
    low = (values - high.astype(np.float64)).astype(ml_dtypes.bfloat16)
    return np.stack([high, low])


def lane_tables():
    ids = np.arange(lane_count)
    angles = 2.0 * np.pi * (np.outer(ids, ids) % lane_count) / lane_count
    cos_part, sin_part = np.cos(angles), np.sin(angles)
    forward = np.block([[cos_part, -sin_part], [sin_part, cos_part]])
    inverse = np.block([[cos_part, sin_part], [-sin_part, cos_part]]) / base_length
    return host_split(forward), host_split(inverse)


def twiddle_table(parts):
    angles = 2.0 * np.pi * np.outer(np.arange(parts), np.arange(lane_count)) / base_length
    return np.stack([np.cos(angles), np.sin(angles)]).astype(np.float32)


def lane_order(width):
    strands = width // lane_count
    order = np.zeros((width, width), np.float32)
    for sample in range(width):
        order[sample, (sample % strands) * lane_count + sample // strands] = 1.0
    return order.astype(ml_dtypes.bfloat16)


def times_root(value, step, count, direction):
    real_part, imaginary = value
    if step == 0:
        return value
    if 4 * step == count:
        return (-imaginary, real_part) if direction > 0 else (imaginary, -real_part)
    cosine = math.cos(2.0 * math.pi * step / count)
    sine = direction * math.sin(2.0 * math.pi * step / count)
    return (real_part * cosine - imaginary * sine, real_part * sine + imaginary * cosine)


def short_transform(values, direction):
    count = len(values)
    if count == 1:
        return values
    even = short_transform(values[0::2], direction)
    odd = short_transform(values[1::2], direction)
    low, high = [], []
    for step in range(count // 2):
        turned = times_root(odd[step], step, count, direction)
        low.append((even[step][0] + turned[0], even[step][1] + turned[1]))
        high.append((even[step][0] - turned[0], even[step][1] - turned[1]))
    return low + high


def unit_circle(index):
    quarter = chirp_modulus // 4
    turns = lax.shift_right_arithmetic(index + quarter // 2, quarter.bit_length() - 1)
    theta = (index - turns * quarter).astype(jnp.float32) * (2.0 * math.pi / chirp_modulus)
    square = theta * theta
    sine = theta * (1.0 + square * (-1 / 6 + square * (1 / 120 + square * (-1 / 5040 + square * (1 / 362880)))))
    cosine = 1.0 + square * (-1 / 2 + square * (1 / 24 + square * (-1 / 720 + square * (1 / 40320 - square / 3628800))))
    swap = (turns & 1) == 1
    first = jnp.where(swap, sine, cosine)
    second = jnp.where(swap, cosine, sine)
    first = jnp.where(((turns + 1) & 2) == 2, -first, first)
    second = jnp.where((turns & 2) == 2, -second, second)
    return first, second


def dot(left, right):
    return jnp.dot(left, right, preferred_element_type=jnp.float32)


def dot_split(left, table_ref):
    high, low = split_pair(left)
    return dot(high, table_ref[0]) + dot(low, table_ref[0]) + dot(high, table_ref[1])


def filter_kernel(
    stn_count, parts, sent_ref, weight_ref, rate_ref, order_ref, back_ref, fwd_ref, inv_ref, twiddle_ref,
    words_ref, peaks_ref, volt_ref, grid_ref, mid_ref, chirp_ref, word_ref, scale_ref,
    in_send, in_recv, out_send, out_recv, copy_sems,
):
    width = volt_ref.shape[2]
    strands = width // lane_count
    beams = rate_ref.shape[0]
    own_beams = beams // stn_count
    rows = 8
    chunk = 8
    part_beams = own_beams // halves
    half_beams = beams // halves
    devices = stn_count * parts
    time_rank = lax.axis_index("tm")
    me = lax.axis_index("stn") * parts + time_rank

    def place(device):
        return (device // parts, device % parts)

    def send_in(target, slot):
        return pltpu.make_async_remote_copy(
            src_ref=sent_ref.at[target],
            dst_ref=volt_ref.at[slot],
            send_sem=in_send.at[target],
            recv_sem=in_recv.at[slot],
            device_id=place(target),
            device_id_type=MESH,
        )

    def views(half, slot):
        some = pl.ds(pl.multiple_of(half * part_beams, part_beams), part_beams)
        return (word_ref.at[slot, some], words_ref.at[slot, some]), (
            scale_ref.at[half, slot], peaks_ref.at[half, slot])

    def send_out(which, half, target, slot):
        return pltpu.make_async_remote_copy(
            src_ref=views(half, target)[which][0],
            dst_ref=views(half, slot)[which][1],
            send_sem=out_send.at[which, half, target],
            recv_sem=out_recv.at[which, half, slot],
            device_id=place(target),
            device_id_type=MESH,
        )

    barrier = pltpu.get_barrier_semaphore()

    @pl.loop(1, devices)
    def _(offset):
        pl.semaphore_signal(
            barrier, inc=1, device_id=place(lax.rem(me + offset, devices)), device_id_type=MESH
        )

    pl.semaphore_wait(barrier, devices - 1)

    @pl.loop(1, devices)
    def _(offset):
        send_in(lax.rem(me + offset, devices), me).start()

    own = pltpu.make_async_copy(sent_ref.at[me], volt_ref.at[me], copy_sems.at[0])
    own.start()

    def regroup(values):
        return jnp.concatenate(
            [
                values[stn * own_beams + half * part_beams : stn * own_beams + (half + 1) * part_beams]
                for half in range(halves)
                for stn in range(stn_count)
            ],
            axis=0,
        )

    weights = weight_ref[...]
    weights = jnp.concatenate([regroup(weights[:beams]), regroup(weights[beams:])], axis=0)
    weight_high, weight_low = split_pair(weights)
    rates = regroup(rate_ref[...])

    @pl.loop(0, parts)
    def _(part):
        column = lax.broadcasted_iota(jnp.int32, (beams, lane_count), 1)
        frequency = part + parts * column
        squares = (frequency * frequency) & (chirp_modulus - 1)
        index = (rates * squares) & (chirp_modulus - 1)
        cosine, sine = unit_circle(index)
        chirp_ref[0, part] = cosine
        chirp_ref[1, part] = sine

    own.wait()

    @pl.loop(0, parts)
    def _(turn):
        part = lax.rem(time_rank + parts - turn, parts)
        for stn in range(stn_count):
            slot = stn * parts + part

            @pl.when(slot != me)
            def _():
                send_in(slot, slot).wait_recv()

        pieces = [volt_ref[stn * parts + part] for stn in range(stn_count)]
        block = dot(jnp.concatenate(pieces, axis=0), order_ref[...]).astype(jnp.bfloat16)
        grid_ref[part] = dot(weight_high, block) + dot(weight_low, block)

    def tile(half, step):
        group, strand = step // strands, step % strands
        first = half * half_beams + group * rows
        return (
            pl.ds(pl.multiple_of(first, rows), rows),
            pl.ds(pl.multiple_of(beams + first, rows), rows),
            pl.ds(pl.multiple_of(strand * lane_count, lane_count), lane_count),
            strand,
        )

    groups = parts // chunk
    row_ids = lax.broadcasted_iota(jnp.int32, (part_beams, lane_count), 0)
    lane_ids = lax.broadcasted_iota(jnp.int32, (part_beams, lane_count), 1)

    @pl.loop(0, halves)
    def _(half):
        upper = pl.ds(pl.multiple_of(half * half_beams, half_beams), half_beams)
        lower = pl.ds(pl.multiple_of(beams + half * half_beams, half_beams), half_beams)

        @pl.loop(0, half_beams // rows * strands)
        def _(step):
            top, bottom, lanes, strand = tile(half, step)
            values = [(grid_ref[p, top, lanes], grid_ref[p, bottom, lanes]) for p in range(parts)]
            for k, (real_part, imaginary) in enumerate(short_transform(values, -1)):
                cosine, sine = twiddle_ref[0, pl.ds(k, 1)], twiddle_ref[1, pl.ds(k, 1)]
                mid_ref[strand, k, top, :lane_count] = real_part * cosine + imaginary * sine
                mid_ref[strand, k, top, lane_count:] = imaginary * cosine - real_part * sine

        @pl.loop(0, strands * groups)
        def _(step):
            strand, first = step // groups, (step % groups) * chunk
            some = pl.ds(first, chunk)
            spectrum = dot_split(
                mid_ref[strand, some, upper].reshape(chunk * half_beams, 2 * lane_count), fwd_ref
            )
            real_part, imaginary = spectrum[:, :lane_count], spectrum[:, lane_count:]
            cosine = chirp_ref[0, some, upper].reshape(chunk * half_beams, lane_count)
            sine = chirp_ref[1, some, upper].reshape(chunk * half_beams, lane_count)
            turned = jnp.concatenate(
                [real_part * cosine + imaginary * sine, imaginary * cosine - real_part * sine], axis=1
            )
            mid_ref[strand, some, upper] = dot_split(turned, inv_ref).reshape(
                chunk, half_beams, 2 * lane_count
            )

        @pl.loop(0, half_beams // rows * strands)
        def _(step):
            top, bottom, lanes, strand = tile(half, step)
            values = []
            for k in range(parts):
                cosine, sine = twiddle_ref[0, pl.ds(k, 1)], twiddle_ref[1, pl.ds(k, 1)]
                real_part = mid_ref[strand, k, top, :lane_count]
                imaginary = mid_ref[strand, k, top, lane_count:]
                values.append(
                    (real_part * cosine - imaginary * sine, real_part * sine + imaginary * cosine)
                )
            for p, (real_part, imaginary) in enumerate(short_transform(values, 1)):
                grid_ref[p, top, lanes] = real_part
                grid_ref[p, bottom, lanes] = imaginary

        @pl.loop(0, parts)
        def _(turn):
            part = lax.rem(time_rank + 1 + turn, parts)
            block = jnp.concatenate([grid_ref[part, upper], grid_ref[part, lower]], axis=0)
            high, low = split_pair(block)
            series = dot(high, back_ref[...]) + dot(low, back_ref[...])
            peak = jnp.maximum(jnp.max(jnp.abs(series), axis=1, keepdims=True), 1e-30)
            codes = jnp.round(series * (code_limit / peak)).astype(jnp.int32)
            words = (codes[:half_beams] << 16) | (codes[half_beams:] & 0xFFFF)
            for stn in range(stn_count):
                slot = stn * parts + part
                first = stn * part_beams
                second = half_beams + first
                word_ref[slot, pl.ds(pl.multiple_of(half * part_beams, part_beams), part_beams)] = words[
                    first : first + part_beams
                ]
                peaks = jnp.where(row_ids == lane_ids, peak[first : first + part_beams], 0.0)
                peaks += jnp.where(
                    row_ids + part_beams == lane_ids, peak[second : second + part_beams], 0.0
                )
                peaks = jnp.sum(peaks, axis=0, keepdims=True)
                scale_ref[half, slot] = jnp.broadcast_to(peaks, scale_ref.shape[2:])

                @pl.when(slot != me)
                def _():
                    for which in range(2):
                        send_out(which, half, slot, me).start()

    own = []
    for half in range(halves):
        for which, (source, target) in enumerate(views(half, me)):
            own.append(pltpu.make_async_copy(source, target, copy_sems.at[1 + 2 * half + which]))
    for copy in own:
        copy.start()
    for copy in own:
        copy.wait()

    @pl.loop(1, devices)
    def _(offset):
        other = lax.rem(me + offset, devices)
        send_in(other, me).wait_send()
        for half in range(halves):
            for which in range(2):
                send_out(which, half, other, me).wait_send()
                send_out(which, half, other, other).wait_recv()


def filter_channel(stn_count, parts, sent, weights, rates):
    devices, inputs, width = sent.shape
    beams = rates.shape[0]
    own_beams = beams // stn_count
    forward, inverse = lane_tables()
    order = lane_order(width)
    vmem = pl.BlockSpec(memory_space=pltpu.VMEM)
    place = pl.BlockSpec(memory_space=pl.ANY)
    words_shape = (devices, own_beams, width)
    peaks_shape = (halves, devices, 8, lane_count)
    return pl.pallas_call(
        functools.partial(filter_kernel, stn_count, parts),
        out_shape=(
            jax.ShapeDtypeStruct(words_shape, jnp.int32),
            jax.ShapeDtypeStruct(peaks_shape, jnp.float32),
        ),
        in_specs=[place] + [vmem] * 7,
        out_specs=(place, place),
        scratch_shapes=[
            pltpu.VMEM((devices, inputs, width), sent.dtype),
            pltpu.VMEM((parts, 2 * beams, width), jnp.float32),
            pltpu.VMEM((width // lane_count, parts, beams, 2 * lane_count), jnp.float32),
            pltpu.VMEM((2, parts, beams, lane_count), jnp.float32),
            pltpu.VMEM(words_shape, jnp.int32),
            pltpu.VMEM(peaks_shape, jnp.float32),
            pltpu.SemaphoreType.DMA((devices,)),
            pltpu.SemaphoreType.DMA((devices,)),
            pltpu.SemaphoreType.DMA((2, halves, devices)),
            pltpu.SemaphoreType.DMA((2, halves, devices)),
            pltpu.SemaphoreType.DMA((1 + 2 * halves,)),
        ],
        compiler_params=pltpu.CompilerParams(
            vmem_limit_bytes=44 * 2**20, collective_id=0, has_side_effects=True
        ),
        name="filter_channel",
    )(
        sent, weights, rates, jnp.asarray(order), jnp.asarray(order.T), jnp.asarray(forward),
        jnp.asarray(inverse), jnp.asarray(twiddle_table(parts)),
    )


def channel_body(voltages, phase_codes, dispersion):
    stn_count, parts = lax.axis_size("stn"), lax.axis_size("tm")
    group_size, _, channels, width = voltages.shape
    station_total, _, beams = phase_codes.shape
    channel = lax.axis_index("stn") * parts + lax.axis_index("tm")
    sent = jnp.transpose(voltages, (2, 0, 1, 3)).reshape(channels, 2 * group_size, width)
    codes = lax.dynamic_index_in_dim(phase_codes, channel, 1, keepdims=False).T
    angles = codes.astype(jnp.float32) * (2.0 * math.pi / phase_levels)
    w_real = jnp.cos(angles) / math.sqrt(station_total)
    w_imaginary = jnp.sin(angles) / math.sqrt(station_total)
    weights = jnp.stack(
        [jnp.stack([w_real, -w_imaginary], axis=-1), jnp.stack([w_imaginary, w_real], axis=-1)]
    ).reshape(2 * beams, 2 * station_total)
    rates = (dispersion * (2 * channels - channel) % chirp_modulus)[:, None]
    words, peaks = filter_channel(stn_count, parts, sent, weights, rates)
    own_beams = beams // stn_count
    codes = jnp.stack([words >> 16, (words << 16) >> 16], axis=1).astype(jnp.float32)
    peaks = peaks[:, :, 0, : 2 * own_beams // halves].reshape(halves, channels, 2, own_beams // halves)
    peaks = jnp.transpose(peaks, (1, 2, 0, 3)).reshape(channels, 2, own_beams, 1)
    steps = peaks * (1.0 / code_limit)
    return jnp.transpose(codes * steps, (2, 1, 0, 3))


def solution(mesh):
    stn_count, parts = mesh.shape["stn"], mesh.shape["tm"]

    def run(voltages, phase_codes, dispersion):
        channels, length = voltages.shape[2:]
        by_channel = channels == stn_count * parts and parts * lane_count == base_length
        by_channel = by_channel and length % base_length == 0
        return jax.shard_map(
            channel_body if by_channel else body,
            mesh=mesh,
            in_specs=(P("stn", None, None, "tm"), P(), P()),
            out_specs=P("stn", None, None, "tm"),
            check_vma=False,
        )(voltages, phase_codes, dispersion)

    return run
```

```python
import functools
import math

import jax
import jax.numpy as jnp
import ml_dtypes
import numpy as np
from jax import lax
from jax.experimental import pallas as pl
from jax.experimental.pallas import tpu as pltpu
from jax.sharding import PartitionSpec as P

chirp_modulus = 4096
phase_levels = 256


def weight_stack(phase_codes, weight_scale):
    angles = phase_codes.astype(jnp.float32) * (2.0 * math.pi / phase_levels)
    w_real = jnp.cos(angles) * weight_scale
    w_imaginary = jnp.sin(angles) * weight_scale
    return jnp.stack([w_real, w_imaginary], axis=1)


def shard_terms(weights, voltages):
    wr_part = weights[:, 0]
    wi_part = weights[:, 1]
    volt_real = voltages[:, 0]
    volt_imaginary = voltages[:, 1]

    def contract(left, right):
        return jnp.einsum(
            "scb,sct->bct",
            left,
            right,
            preferred_element_type=jnp.float32,
            precision=lax.Precision.HIGHEST,
        )

    real_part = contract(wr_part, volt_real) - contract(wi_part, volt_imaginary)
    imaginary = contract(wr_part, volt_imaginary) + contract(wi_part, volt_real)
    return jnp.stack([real_part, imaginary], axis=1)


def angle_pair(row_ids, column_ids, modulus, direction):
    phase_index = row_ids[:, None] * column_ids[None, :] % modulus
    angles = phase_index.astype(jnp.float32) * (direction * 2.0 * math.pi / modulus)
    return (jnp.cos(angles), jnp.sin(angles))


def along_last(real_part, imaginary, tables):
    cos_part, sin_part = tables

    def contract(left, right):
        return jnp.einsum("...n,nk->...k", left, right, precision=lax.Precision.HIGHEST)

    return (
        contract(real_part, cos_part) - contract(imaginary, sin_part),
        contract(real_part, sin_part) + contract(imaginary, cos_part),
    )


def along_second(real_part, imaginary, tables):
    cos_part, sin_part = tables

    def contract(left, right):
        return jnp.einsum("...nl,nk->...kl", left, right, precision=lax.Precision.HIGHEST)

    return (
        contract(real_part, cos_part) - contract(imaginary, sin_part),
        contract(real_part, sin_part) + contract(imaginary, cos_part),
    )


def rotate(real_part, imaginary, tables):
    cos_part, sin_part = tables
    return (
        real_part * cos_part - imaginary * sin_part,
        real_part * sin_part + imaginary * cos_part,
    )


def chirp_pair(dm_values, channel_ids, frequency, length, channel_total):
    centered = jnp.where(frequency < length // 2, frequency, frequency - length)
    squares = centered * centered % chirp_modulus
    chirp_rate = dm_values[:, None] * (2 * channel_total - channel_ids)[None, :] % chirp_modulus
    phase_index = chirp_rate[:, :, None, None] * squares[None, None] % chirp_modulus
    angles = phase_index.astype(jnp.float32) * (-2.0 * math.pi / chirp_modulus)
    return (jnp.cos(angles), jnp.sin(angles))


def body(voltages, phase_codes, dispersion):
    stn_count = lax.axis_size("stn")
    group_size = voltages.shape[0]
    channels = voltages.shape[2]
    local_time = voltages.shape[3]
    beam_total = phase_codes.shape[2]
    station_total = phase_codes.shape[0]
    own_beams = beam_total // stn_count
    own_start = lax.axis_index("stn") * own_beams
    weight_scale = 1.0 / math.sqrt(station_total)
    group_start = lax.axis_index("stn") * group_size
    local_codes = lax.dynamic_slice_in_dim(phase_codes, group_start, group_size, 0)
    weights = weight_stack(local_codes, weight_scale)
    beams = lax.psum_scatter(shard_terms(weights, voltages), "stn", scatter_dimension=0, tiled=True)
    time_shards = lax.axis_size("tm")
    time_rank = lax.axis_index("tm")
    length = time_shards * local_time
    shard_ids = jnp.arange(time_shards, dtype=jnp.int32)
    sample_ids = jnp.arange(local_time, dtype=jnp.int32)
    dm_values = lax.dynamic_slice_in_dim(dispersion, own_start, own_beams)
    inverse_length = 1.0 / length
    column_width = local_time // time_shards
    layout = beams.reshape(own_beams, 2, channels, 1, local_time)
    layout = lax.all_to_all(layout, "tm", split_axis=4, concat_axis=3, tiled=True)
    real_part, imaginary = along_second(
        layout[:, 0], layout[:, 1], angle_pair(shard_ids, shard_ids, time_shards, -1.0)
    )
    global_samples = time_rank * column_width + jnp.arange(column_width, dtype=jnp.int32)
    real_part, imaginary = rotate(
        real_part, imaginary, angle_pair(shard_ids, global_samples, length, -1.0)
    )
    layout = lax.all_to_all(
        jnp.stack([real_part, imaginary], axis=1), "tm", split_axis=3, concat_axis=4, tiled=True
    )
    real_part, imaginary = along_last(
        layout[:, 0], layout[:, 1], angle_pair(sample_ids, sample_ids, local_time, -1.0)
    )
    frequency = time_rank + time_shards * sample_ids[None, :]
    channel_ids = jnp.arange(channels, dtype=jnp.int32)
    real_part, imaginary = rotate(
        real_part, imaginary, chirp_pair(dm_values, channel_ids, frequency, length, channels)
    )
    real_part, imaginary = along_last(
        real_part, imaginary, angle_pair(sample_ids, sample_ids, local_time, 1.0)
    )
    rank_ids = jnp.reshape(time_rank, (1,))
    real_part, imaginary = rotate(
        real_part, imaginary, angle_pair(rank_ids, sample_ids, length, 1.0)
    )
    layout = lax.all_to_all(
        jnp.stack([real_part, imaginary], axis=1), "tm", split_axis=4, concat_axis=3, tiled=True
    )
    real_part, imaginary = along_second(
        layout[:, 0], layout[:, 1], angle_pair(shard_ids, shard_ids, time_shards, 1.0)
    )
    layout = jnp.stack([real_part, imaginary], axis=1) * inverse_length
    layout = lax.all_to_all(layout, "tm", split_axis=3, concat_axis=4, tiled=True)
    return layout.reshape(own_beams, 2, channels, local_time)


MESH = pl.DeviceIdType.MESH
base_length = chirp_modulus // 2
lane_count = 128
code_limit = 32766.0
halves = 2


def split_pair(values):
    high = values.astype(jnp.bfloat16)
    return high, (values - high.astype(jnp.float32)).astype(jnp.bfloat16)


def host_split(values):
    high = values.astype(ml_dtypes.bfloat16)
    low = (values - high.astype(np.float64)).astype(ml_dtypes.bfloat16)
    return np.stack([high, low])


def lane_tables():
    ids = np.arange(lane_count)
    angles = 2.0 * np.pi * (np.outer(ids, ids) % lane_count) / lane_count
    cos_part, sin_part = np.cos(angles), np.sin(angles)
    forward = np.block([[cos_part, -sin_part], [sin_part, cos_part]])
    inverse = np.block([[cos_part, sin_part], [-sin_part, cos_part]]) / base_length
    return host_split(forward), host_split(inverse)


def twiddle_table(parts):
    angles = 2.0 * np.pi * np.outer(np.arange(parts), np.arange(lane_count)) / base_length
    return np.stack([np.cos(angles), np.sin(angles)]).astype(np.float32)


def lane_order(width):
    strands = width // lane_count
    order = np.zeros((width, width), np.float32)
    for sample in range(width):
        order[sample, (sample % strands) * lane_count + sample // strands] = 1.0
    return order.astype(ml_dtypes.bfloat16)


def times_root(value, step, count, direction):
    real_part, imaginary = value
    if step == 0:
        return value
    if 4 * step == count:
        return (-imaginary, real_part) if direction > 0 else (imaginary, -real_part)
    cosine = math.cos(2.0 * math.pi * step / count)
    sine = direction * math.sin(2.0 * math.pi * step / count)
    return (real_part * cosine - imaginary * sine, real_part * sine + imaginary * cosine)


def short_transform(values, direction):
    count = len(values)
    if count == 1:
        return values
    even = short_transform(values[0::2], direction)
    odd = short_transform(values[1::2], direction)
    low, high = [], []
    for step in range(count // 2):
        turned = times_root(odd[step], step, count, direction)
        low.append((even[step][0] + turned[0], even[step][1] + turned[1]))
        high.append((even[step][0] - turned[0], even[step][1] - turned[1]))
    return low + high


def unit_circle(index):
    quarter = chirp_modulus // 4
    turns = lax.shift_right_arithmetic(index + quarter // 2, quarter.bit_length() - 1)
    theta = (index - turns * quarter).astype(jnp.float32) * (2.0 * math.pi / chirp_modulus)
    square = theta * theta
    sine = theta * (1.0 + square * (-1 / 6 + square * (1 / 120 + square * (-1 / 5040 + square * (1 / 362880)))))
    cosine = 1.0 + square * (-1 / 2 + square * (1 / 24 + square * (-1 / 720 + square * (1 / 40320 - square / 3628800))))
    swap = (turns & 1) == 1
    first = jnp.where(swap, sine, cosine)
    second = jnp.where(swap, cosine, sine)
    first = jnp.where(((turns + 1) & 2) == 2, -first, first)
    second = jnp.where((turns & 2) == 2, -second, second)
    return first, second


def dot(left, right):
    return jnp.dot(left, right, preferred_element_type=jnp.float32)


def dot_split(left, table_ref):
    high, low = split_pair(left)
    return dot(high, table_ref[0]) + dot(low, table_ref[0]) + dot(high, table_ref[1])


def filter_kernel(
    stn_count, parts, sent_ref, weight_ref, rate_ref, order_ref, back_ref, fwd_ref, inv_ref, twiddle_ref,
    words_ref, peaks_ref, volt_ref, grid_ref, mid_ref, chirp_ref, word_ref, scale_ref,
    in_send, in_recv, out_send, out_recv, copy_sems,
):
    width = volt_ref.shape[2]
    strands = width // lane_count
    beams = rate_ref.shape[0]
    own_beams = beams // stn_count
    rows = 8
    chunk = min(parts, 2 * lane_count * halves // rate_ref.shape[0])
    part_beams = own_beams // halves
    half_beams = beams // halves
    devices = stn_count * parts
    time_rank = lax.axis_index("tm")
    me = lax.axis_index("stn") * parts + time_rank

    def place(device):
        return (device // parts, device % parts)

    def send_in(target, slot):
        return pltpu.make_async_remote_copy(
            src_ref=sent_ref.at[target],
            dst_ref=volt_ref.at[slot],
            send_sem=in_send.at[target],
            recv_sem=in_recv.at[slot],
            device_id=place(target),
            device_id_type=MESH,
        )

    def views(half, slot):
        some = pl.ds(pl.multiple_of(half * part_beams, part_beams), part_beams)
        return (word_ref.at[slot, some], words_ref.at[slot, some]), (
            scale_ref.at[half, slot], peaks_ref.at[half, slot])

    def send_out(which, half, target, slot):
        return pltpu.make_async_remote_copy(
            src_ref=views(half, target)[which][0],
            dst_ref=views(half, slot)[which][1],
            send_sem=out_send.at[which, half, target],
            recv_sem=out_recv.at[which, half, slot],
            device_id=place(target),
            device_id_type=MESH,
        )

    barrier = pltpu.get_barrier_semaphore()

    @pl.loop(1, devices)
    def _(offset):
        pl.semaphore_signal(
            barrier, inc=1, device_id=place(lax.rem(me + offset, devices)), device_id_type=MESH
        )

    pl.semaphore_wait(barrier, devices - 1)

    @pl.loop(1, devices)
    def _(offset):
        send_in(lax.rem(me + offset, devices), me).start()

    own = pltpu.make_async_copy(sent_ref.at[me], volt_ref.at[me], copy_sems.at[0])
    own.start()

    def regroup(values):
        return jnp.concatenate(
            [
                values[stn * own_beams + half * part_beams : stn * own_beams + (half + 1) * part_beams]
                for half in range(halves)
                for stn in range(stn_count)
            ],
            axis=0,
        )

    weights = weight_ref[...]
    weights = jnp.concatenate([regroup(weights[:beams]), regroup(weights[beams:])], axis=0)
    weight_high, weight_low = split_pair(weights)
    rates = regroup(rate_ref[...])

    @pl.loop(0, parts)
    def _(part):
        column = lax.broadcasted_iota(jnp.int32, (beams, lane_count), 1)
        frequency = part + parts * column
        squares = (frequency * frequency) & (chirp_modulus - 1)
        index = (rates * squares) & (chirp_modulus - 1)
        cosine, sine = unit_circle(index)
        chirp_ref[0, part] = cosine
        chirp_ref[1, part] = sine

    own.wait()

    @pl.loop(0, parts)
    def _(turn):
        part = lax.rem(time_rank + parts - turn, parts)
        for stn in range(stn_count):
            slot = stn * parts + part

            @pl.when(slot != me)
            def _():
                send_in(slot, slot).wait_recv()

        pieces = [volt_ref[stn * parts + part] for stn in range(stn_count)]
        block = dot(jnp.concatenate(pieces, axis=0), order_ref[...]).astype(jnp.bfloat16)
        grid_ref[part] = dot(weight_high, block) + dot(weight_low, block)

    def tile(half, step):
        group, strand = step // strands, step % strands
        first = half * half_beams + group * rows
        return (
            pl.ds(pl.multiple_of(first, rows), rows),
            pl.ds(pl.multiple_of(beams + first, rows), rows),
            pl.ds(pl.multiple_of(strand * lane_count, lane_count), lane_count),
            strand,
        )

    groups = parts // chunk
    row_ids = lax.broadcasted_iota(jnp.int32, (part_beams, lane_count), 0)
    lane_ids = lax.broadcasted_iota(jnp.int32, (part_beams, lane_count), 1)

    @pl.loop(0, halves)
    def _(half):
        upper = pl.ds(pl.multiple_of(half * half_beams, half_beams), half_beams)
        lower = pl.ds(pl.multiple_of(beams + half * half_beams, half_beams), half_beams)

        @pl.loop(0, half_beams // rows * strands)
        def _(step):
            top, bottom, lanes, strand = tile(half, step)
            values = [(grid_ref[p, top, lanes], grid_ref[p, bottom, lanes]) for p in range(parts)]
            for k, (real_part, imaginary) in enumerate(short_transform(values, -1)):
                cosine, sine = twiddle_ref[0, pl.ds(k, 1)], twiddle_ref[1, pl.ds(k, 1)]
                mid_ref[strand, k, top, :lane_count] = real_part * cosine + imaginary * sine
                mid_ref[strand, k, top, lane_count:] = imaginary * cosine - real_part * sine

        @pl.loop(0, strands * groups)
        def _(step):
            strand, first = step // groups, (step % groups) * chunk
            some = pl.ds(first, chunk)
            spectrum = dot_split(
                mid_ref[strand, some, upper].reshape(chunk * half_beams, 2 * lane_count), fwd_ref
            )
            real_part, imaginary = spectrum[:, :lane_count], spectrum[:, lane_count:]
            cosine = chirp_ref[0, some, upper].reshape(chunk * half_beams, lane_count)
            sine = chirp_ref[1, some, upper].reshape(chunk * half_beams, lane_count)
            turned = jnp.concatenate(
                [real_part * cosine + imaginary * sine, imaginary * cosine - real_part * sine], axis=1
            )
            mid_ref[strand, some, upper] = dot_split(turned, inv_ref).reshape(
                chunk, half_beams, 2 * lane_count
            )

        @pl.loop(0, half_beams // rows * strands)
        def _(step):
            top, bottom, lanes, strand = tile(half, step)
            values = []
            for k in range(parts):
                cosine, sine = twiddle_ref[0, pl.ds(k, 1)], twiddle_ref[1, pl.ds(k, 1)]
                real_part = mid_ref[strand, k, top, :lane_count]
                imaginary = mid_ref[strand, k, top, lane_count:]
                values.append(
                    (real_part * cosine - imaginary * sine, real_part * sine + imaginary * cosine)
                )
            for p, (real_part, imaginary) in enumerate(short_transform(values, 1)):
                grid_ref[p, top, lanes] = real_part
                grid_ref[p, bottom, lanes] = imaginary

        @pl.loop(0, parts)
        def _(turn):
            part = lax.rem(time_rank + 1 + turn, parts)
            block = jnp.concatenate([grid_ref[part, upper], grid_ref[part, lower]], axis=0)
            high, low = split_pair(block)
            series = dot(high, back_ref[...]) + dot(low, back_ref[...])
            peak = jnp.maximum(jnp.max(jnp.abs(series), axis=1, keepdims=True), 1e-30)
            codes = jnp.round(series * (code_limit / peak)).astype(jnp.int32)
            words = (codes[:half_beams] << 16) | (codes[half_beams:] & 0xFFFF)
            for stn in range(stn_count):
                slot = stn * parts + part
                first = stn * part_beams
                second = half_beams + first
                word_ref[slot, pl.ds(pl.multiple_of(half * part_beams, part_beams), part_beams)] = words[
                    first : first + part_beams
                ]
                peaks = jnp.where(row_ids == lane_ids, peak[first : first + part_beams], 0.0)
                peaks += jnp.where(
                    row_ids + part_beams == lane_ids, peak[second : second + part_beams], 0.0
                )
                peaks = jnp.sum(peaks, axis=0, keepdims=True)
                scale_ref[half, slot] = peaks

                @pl.when(slot != me)
                def _():
                    for which in range(2):
                        send_out(which, half, slot, me).start()

    own = []
    for half in range(halves):
        for which, (source, target) in enumerate(views(half, me)):
            own.append(pltpu.make_async_copy(source, target, copy_sems.at[1 + 2 * half + which]))
    for copy in own:
        copy.start()
    for copy in own:
        copy.wait()

    @pl.loop(1, devices)
    def _(offset):
        other = lax.rem(me + offset, devices)
        send_in(other, me).wait_send()
        for half in range(halves):
            for which in range(2):
                send_out(which, half, other, me).wait_send()
                send_out(which, half, other, other).wait_recv()


def filter_channel(stn_count, parts, sent, weights, rates):
    devices, inputs, width = sent.shape
    beams = rates.shape[0]
    own_beams = beams // stn_count
    forward, inverse = lane_tables()
    order = lane_order(width)
    vmem = pl.BlockSpec(memory_space=pltpu.VMEM)
    place = pl.BlockSpec(memory_space=pl.ANY)
    words_shape = (devices, own_beams, width)
    peaks_shape = (halves, devices, 1, lane_count)
    return pl.pallas_call(
        functools.partial(filter_kernel, stn_count, parts),
        out_shape=(
            jax.ShapeDtypeStruct(words_shape, jnp.int32),
            jax.ShapeDtypeStruct(peaks_shape, jnp.float32),
        ),
        in_specs=[place] + [vmem] * 7,
        out_specs=(place, place),
        scratch_shapes=[
            pltpu.VMEM((devices, inputs, width), sent.dtype),
            pltpu.VMEM((parts, 2 * beams, width), jnp.float32),
            pltpu.VMEM((width // lane_count, parts, beams, 2 * lane_count), jnp.float32),
            pltpu.VMEM((2, parts, beams, lane_count), jnp.float32),
            pltpu.VMEM(words_shape, jnp.int32),
            pltpu.VMEM(peaks_shape, jnp.float32),
            pltpu.SemaphoreType.DMA((devices,)),
            pltpu.SemaphoreType.DMA((devices,)),
            pltpu.SemaphoreType.DMA((2, halves, devices)),
            pltpu.SemaphoreType.DMA((2, halves, devices)),
            pltpu.SemaphoreType.DMA((1 + 2 * halves,)),
        ],
        compiler_params=pltpu.CompilerParams(
            vmem_limit_bytes=44 * 2**20, collective_id=0, has_side_effects=True
        ),
        name="filter_channel",
    )(
        sent, weights, rates, jnp.asarray(order), jnp.asarray(order.T), jnp.asarray(forward),
        jnp.asarray(inverse), jnp.asarray(twiddle_table(parts)),
    )


def channel_body(voltages, phase_codes, dispersion):
    stn_count, parts = lax.axis_size("stn"), lax.axis_size("tm")
    group_size, _, channels, width = voltages.shape
    station_total, _, beams = phase_codes.shape
    channel = lax.axis_index("stn") * parts + lax.axis_index("tm")
    sent = jnp.transpose(voltages, (2, 0, 1, 3)).reshape(channels, 2 * group_size, width)
    codes = lax.dynamic_index_in_dim(phase_codes, channel, 1, keepdims=False).T
    angles = codes.astype(jnp.float32) * (2.0 * math.pi / phase_levels)
    w_real = jnp.cos(angles) / math.sqrt(station_total)
    w_imaginary = jnp.sin(angles) / math.sqrt(station_total)
    weights = jnp.stack(
        [jnp.stack([w_real, -w_imaginary], axis=-1), jnp.stack([w_imaginary, w_real], axis=-1)]
    ).reshape(2 * beams, 2 * station_total)
    rates = (dispersion * (2 * channels - channel) % chirp_modulus)[:, None]
    words, peaks = filter_channel(stn_count, parts, sent, weights, rates)
    own_beams = beams // stn_count
    codes = jnp.stack([words >> 16, (words << 16) >> 16], axis=1).astype(jnp.float32)
    peaks = peaks[:, :, 0, : 2 * own_beams // halves].reshape(halves, channels, 2, own_beams // halves)
    peaks = jnp.transpose(peaks, (1, 2, 0, 3)).reshape(channels, 2, own_beams, 1)
    steps = peaks * (1.0 / code_limit)
    return jnp.transpose(codes * steps, (2, 1, 0, 3))


def solution(mesh):
    stn_count, parts = mesh.shape["stn"], mesh.shape["tm"]

    def run(voltages, phase_codes, dispersion):
        channels, length = voltages.shape[2:]
        by_channel = channels == stn_count * parts and parts * lane_count == base_length
        by_channel = by_channel and length % base_length == 0
        return jax.shard_map(
            channel_body if by_channel else body,
            mesh=mesh,
            in_specs=(P("stn", None, None, "tm"), P(), P()),
            out_specs=P("stn", None, None, "tm"),
            check_vma=False,
        )(voltages, phase_codes, dispersion)

    return run
```
